32 devices in a mesh: gx: 2 (over y), gy: 4 (over x, core), gz: 4 (over z).
Axes of the slice: x: 2, y: 2, z: 4, core: 2. Of those that a mesh axis runs over, the one named last changes fastest.
Arguments:
- right_side: float32 [32, 64, 256], P('gx', 'gy', 'gz'), may hold values from -8 to 8
- diagonal: float32 [32, 64, 256], P('gx', 'gy', 'gz'), may hold values from 0.001 to 0.01
Outputs:
- pressure: float32 [32, 64, 256], P('gx', 'gy', 'gz')
- residual: float32 [32, 64, 256], P('gx', 'gy', 'gz')
The draws below stay inside these ranges and needn't reach their ends.
All inputs are finite; a program needn't handle non-finite values.
Results may differ from the reference program's by a relative error of at most 0.0003.
Values sent between devices are 32-bit elements; how exact they have to be, the bound alone decides.
A program may use at most 64 MiB of HBM per device.

```python
import math
import jax
import jax.numpy as jnp

DEGREE = 3
NX = 32
NY = 64
NZ = 256


def draw_right_side(key, part):
    key = jax.random.fold_in(key, 11)
    return jnp.clip(jax.random.normal(key, (NX, NY, NZ), jnp.float32), -5.0, 5.0)


def steps_of(own_key, extent, cuts, least, high):
    def one(axis_at, parts):
        steps = jax.random.uniform(jax.random.fold_in(jax.random.fold_in(own_key, 6), axis_at), (parts,), jnp.float32, least / len(cuts), high / len(cuts))
        return jnp.repeat(jnp.exp(steps), extent[axis_at] // parts).reshape((-1,) + (1,) * (len(extent) - axis_at - 1))

    gain = one(*cuts[0])
    for cut in cuts[1:]:
        gain = gain * one(*cut)
    return gain


def setup_inputs(seed: int = 0) -> dict:
    arg_keys = jax.random.split(jax.random.key(seed), 3)
    right_side = draw_right_side(jax.random.fold_in(arg_keys[2], 71), 0)
    diagonal = jnp.clip(jnp.exp(math.log(0.01) - 2.30258502 * jax.random.uniform(arg_keys[1], (NX, NY, NZ), jnp.float32) ** steps_of(arg_keys[1], (NX, NY, NZ), ((0, 2), (1, 4), (2, 4)), -0.2, 0.2)), 0.001, 0.01)
    return {"right_side": right_side, "diagonal": diagonal}


CHEB_LOW = 0.3
CHEB_HIGH = 2.0


def beside_sum(padded):
    neighbour_sum = padded[2:, 1:-1, 1:-1] + padded[:-2, 1:-1, 1:-1]
    neighbour_sum = neighbour_sum + padded[1:-1, 2:, 1:-1] + padded[1:-1, :-2, 1:-1]
    neighbour_sum = neighbour_sum + padded[1:-1, 1:-1, 2:] + padded[1:-1, 1:-1, :-2]
    return neighbour_sum


def stencil(values, added):
    return (6.0 + added) * values - beside_sum(jnp.pad(values, 1))


def restrict(values):
    first_len, second_len, third_len = values.shape
    blocks = values.reshape(first_len // 2, 2, second_len // 2, 2, third_len // 2, 2)
    return jnp.mean(blocks, axis=(1, 3, 5)) * 4.0


def prolong(values):
    first_len, second_len, third_len = values.shape
    widened = jnp.broadcast_to(values[:, None, :, None, :, None], (first_len, 2, second_len, 2, third_len, 2))
    return widened.reshape(2 * first_len, 2 * second_len, 2 * third_len)


def smooth(source, initial, added, operator, want_residual):
    inverse = 1.0 / (6.0 + added)
    middle = 0.5 * (CHEB_HIGH + CHEB_LOW)
    spread_half = 0.5 * (CHEB_HIGH - CHEB_LOW)
    sigma_one = middle / spread_half
    ratio_old = 1.0 / sigma_one
    if initial is None:
        residual = source
        update = inverse * residual / middle
        iterate = update
    else:
        residual = source - operator(initial, added)
        update = inverse * residual / middle
        iterate = initial + update
    for sweep in range(DEGREE - 1):
        residual = residual - operator(update, added)
        ratio_new = 1.0 / (2.0 * sigma_one - ratio_old)
        update = (ratio_new * ratio_old) * update + (2.0 * ratio_new / spread_half) * inverse * residual
        iterate = iterate + update
        ratio_old = ratio_new
    if want_residual:
        residual = residual - operator(update, added)
    return iterate, residual


def reference(right_side, diagonal):
    shifts = [diagonal]
    for tier_index in range(4):
        shifts.append(restrict(shifts[-1]))

    def cycle(tier_index, source):
        if tier_index == 4:
            iterate, unused = smooth(source, None, shifts[4], stencil, False)
            return iterate
        iterate, residual = smooth(source, None, shifts[tier_index], stencil, True)
        iterate = iterate + prolong(cycle(tier_index + 1, restrict(residual)))
        iterate, unused = smooth(source, iterate, shifts[tier_index], stencil, False)
        return iterate

    pressure = cycle(0, right_side)
    return pressure, right_side - stencil(pressure, diagonal)
```

```python
import functools
import jax
import jax.numpy as jnp
from jax import lax
from jax.experimental import pallas as pl
from jax.experimental.pallas import tpu as pltpu
from jax.sharding import PartitionSpec as P

CHEB_LOW = 0.3
CHEB_HIGH = 2.0
MIDDLE = 0.5 * (CHEB_HIGH + CHEB_LOW)
HALF = 0.5 * (CHEB_HIGH - CHEB_LOW)
SIGMA = MIDDLE / HALF
Q0 = 1.0 / SIGMA
Q1 = 1.0 / (2.0 * SIGMA - Q0)
Q2 = 1.0 / (2.0 * SIGMA - Q1)
STEP0 = (0.0, 1.0 / MIDDLE)
STEP1 = (Q1 * Q0, 2.0 * Q1 / HALF)
STEP2 = (Q2 * Q1, 2.0 * Q2 / HALF)

MESH = pl.DeviceIdType.MESH
HX = 6
BF = jnp.bfloat16
F32 = jnp.float32


def ones_where(condition, value=1.0):
    return jnp.where(condition, value, 0.0).astype(BF)


def iota(shape, dim):
    return lax.broadcasted_iota(jnp.int32, shape, dim)


def split(values):
    high = values.astype(BF)
    return high, (values - high.astype(F32)).astype(BF)


def mm(values, matrix):
    high, low = split(values)
    return jnp.dot(high, matrix, preferred_element_type=F32) + jnp.dot(
        low, matrix, preferred_element_type=F32
    )


def mm_left(matrix, values):
    high, low = split(values)
    return jnp.dot(matrix, high, preferred_element_type=F32) + jnp.dot(
        matrix, low, preferred_element_type=F32
    )


class Level:
    def __init__(self, refs):
        self.r, self.diag, self.inv, self.v, self.d0, self.d1 = refs
        self.planes, self.rows, self.lanes = self.r.shape

    def loop(self, body, unroll):
        count = self.planes
        while count % unroll:
            unroll -= 1

        def step(k, carry):
            for u in range(unroll):
                body(k * unroll + u)
            return carry

        lax.fori_loop(0, count // unroll, step, 0)

    def clear(self):
        zeros = jnp.zeros(self.d0.shape[1:], F32)

        def step(x, carry):
            self.d0[x] = zeros
            self.d1[x] = zeros
            return carry

        lax.fori_loop(0, self.d0.shape[0], step, 0)

    def init(self, source, added, mask, plane_ok=None, unroll=2):
        def body(x):
            f = source(x)
            diag = 6.0 + added(x)
            inv = mask / diag
            if plane_ok is not None:
                inv = inv * plane_ok(x)
            d = inv * f * (1.0 / MIDDLE)
            self.r[x] = f
            self.diag[x] = diag
            self.inv[x] = inv
            self.v[x] = d
            self.d0[x + 1, 8 : 8 + self.rows] = d

        self.loop(body, unroll)

    def sweep(self, old, new, step, unroll=2, add_old=False):
        rows = self.rows

        def body(x):
            d = old[x + 1, 8 : 8 + rows]
            beside = old[x, 8 : 8 + rows] + old[x + 2, 8 : 8 + rows]
            beside = beside + old[x + 1, 7 : 7 + rows] + old[x + 1, 9 : 9 + rows]
            beside = beside + pltpu.roll(d, 1, 1) + pltpu.roll(d, self.lanes - 1, 1)
            r = self.r[x] - self.diag[x] * d + beside
            self.r[x] = r
            if step is None:
                return
            keep, gain = step
            fresh = gain * (self.inv[x] * r)
            if keep:
                fresh = keep * d + fresh
            new[x + 1, 8 : 8 + rows] = fresh
            self.v[x] = self.v[x] + (fresh + d if add_old else fresh)

        self.loop(body, unroll)

    def down(self, want_residual=True, unroll=2):
        self.sweep(self.d0, self.d1, STEP1, unroll)
        self.sweep(self.d1, self.d0, STEP2, unroll)
        if want_residual:
            self.sweep(self.d0, None, None, unroll)

    def up(self, want_residual=False, unroll=2):
        self.sweep(self.d0, self.d1, STEP0, unroll, add_old=True)
        self.sweep(self.d1, self.d0, STEP1, unroll)
        self.sweep(self.d0, self.d1, STEP2, unroll)
        if want_residual:
            self.sweep(self.d1, None, None, unroll)


def kernel(counts, f_ref, a_ref, p_ref, e_ref, turned, window, near_a, near_f, own_a, own_f,
           pack, gathered, whole_f, whole_a, f3, a3, f4, a4, *rest):
    gx, gy, gz = counts
    bx, by, bz = f_ref.shape
    devices = gx * gy * gz
    fine, mid, two, three, four = [Level(rest[6 * k : 6 * k + 6]) for k in range(5)]
    z_send, z_recv, w_send, w_recv, a_send, a_recv, f_send, f_recv, g_send, g_recv = rest[30:]
    me_x = lax.axis_index("gx")
    me_y = lax.axis_index("gy")
    me_z = lax.axis_index("gz")
    small_x = gx <= 2
    at_x = HX * me_x if small_x else HX
    at_one = (bx // 2) * me_x if small_x else bx // 2
    half_x, half_y, half_z = bx // 2, by // 2, bz // 2

    turned[...] = jnp.zeros_like(turned)
    padding = jnp.zeros((bx * by, 128 - bz), F32)
    for k, ref in enumerate((f_ref, a_ref)):
        flat = jnp.concatenate([ref[...].reshape(bx * by, bz), padding], axis=1)
        turned[0:bz, k * bx * by : (k + 1) * bx * by] = flat.T[0:bz]
    for ref in (near_a, near_f, whole_f, whole_a, f4, a4):
        ref[...] = jnp.zeros_like(ref)

    def clear_window(x, carry):
        window[0, x] = jnp.zeros(window.shape[2:], F32)
        window[1, x] = jnp.zeros(window.shape[2:], F32)
        return carry

    lax.fori_loop(0, window.shape[1], clear_window, 0)

    barrier = pltpu.get_barrier_semaphore()
    flat_me = (me_x * gy + me_y) * gz + me_z

    def place(k):
        other = lax.rem(flat_me + k, devices)
        return (lax.div(other, gy * gz), lax.rem(lax.div(other, gz), gy), lax.rem(other, gz))

    def greet(k, carry):
        pl.semaphore_signal(barrier, inc=1, device_id=place(k), device_id_type=MESH)
        return carry

    lax.fori_loop(1, devices, greet, 0)
    pl.semaphore_wait(barrier, devices - 1)

    def z_copy(way):
        src = turned.at[bz - 8 : bz] if way else turned.at[0:8]
        dst = turned.at[120:128] if way else turned.at[bz : bz + 8]
        return pltpu.make_async_remote_copy(
            src_ref=src, dst_ref=dst, send_sem=z_send.at[way], recv_sem=z_recv.at[way],
            device_id=(me_x, me_y, me_z + (1 if way else -1)), device_id_type=MESH)

    has_low, has_high = me_z > 0, me_z < gz - 1
    pl.when(has_high)(lambda: z_copy(1).start())
    pl.when(has_low)(lambda: z_copy(0).start())

    group = iota((4 * 128, 128), 0) // 128
    inner = iota((4 * 128, 128), 0) % 128
    column = iota((4 * 128, 128), 1)
    to_one = ones_where((column == group * 32 + inner // 2) & (inner < bz), 0.5)
    rows_one = ones_where(iota((half_y, by), 1) // 2 == iota((half_y, by), 0))

    def pack_one(plane, out):
        for q in range(half_x // 4):
            sums = jnp.concatenate(
                [plane(2 * (4 * q + j)) + plane(2 * (4 * q + j) + 1) for j in range(4)], axis=1)
            out[q] = mm_left(rows_one, mm(sums, to_one))

    pad_plane = jnp.zeros((by, 128 - bz), F32)
    pack_one(lambda x: jnp.concatenate([a_ref[x], pad_plane], axis=1), own_a)

    offsets_x = (0,) if gx == 1 else ((0, 2) if gx == 2 else (-1, 0, 1))

    def around():
        for ox in offsets_x:
            for oy in (-1, 0, 1):
                for oz in (-1, 0, 1):
                    if (ox, oy, oz) != (0, 0, 0):
                        yield ox, oy, oz

    def beside(ox, oy, oz):
        tx = me_x if ox == 0 else (1 - me_x if ox == 2 else me_x + ox)
        ty, tz = me_y + oy, me_z + oz
        there = None
        tests = []
        if abs(ox) == 1:
            tests.append((tx >= 0) & (tx < gx))
        if oy:
            tests.append(ty >= 0 if oy < 0 else ty < gy)
        if oz:
            tests.append(tz >= 0 if oz < 0 else tz < gz)
        for test in tests:
            there = test if there is None else there & test
        return (tx, ty, tz), there

    def guarded(there, act):
        if there is None:
            act()
        else:
            pl.when(there)(act)

    def brick_copy(offset, own, near, send, recv, arriving):
        ox, oy, oz = offset
        target, there = beside(ox, oy, oz)
        if arriving:
            slot_x = target[0] if small_x else 1 + ox
            slot = (slot_x * 3 + 1 + oy) * 3 + 1 + oz
        else:
            slot_x = me_x if small_x else 1 - ox
            slot = (slot_x * 3 + 1 - oy) * 3 + 1 - oz
        home = ((offsets_x.index(ox)) * 3 + 1 + oy) * 3 + 1 + oz
        copy = pltpu.make_async_remote_copy(
            src_ref=own, dst_ref=near.at[slot], send_sem=send.at[home], recv_sem=recv.at[slot],
            device_id=target, device_id_type=MESH)
        return copy, there

    def bricks(own, near, send, recv, what):
        for offset in around():
            copy, there = brick_copy(offset, own, near, send, recv, what == "recv")
            act = {"start": copy.start, "recv": copy.wait_recv, "send": copy.wait_send}[what]
            guarded(there, act)

    bricks(own_a, near_a, a_send, a_recv, "start")

    to_two = ones_where((column == group * 16 + inner // 2) & (inner < half_z), 0.5)
    to_two_a = ones_where((column == 64 + group * 16 + inner // 2) & (inner < half_z), 0.5)
    rows_two = ones_where(iota((half_y // 2, half_y), 1) // 2 == iota((half_y // 2, half_y), 0))
    lane = iota((8, 128), 1)

    def brick_plane(own, x):
        moved = own[x // 4]
        if x % 4:
            moved = pltpu.roll(moved, 128 - 32 * (x % 4), 1)
        return moved

    sums = jnp.concatenate(
        [brick_plane(own_a, 2 * i) + brick_plane(own_a, 2 * i + 1) for i in range(4)], axis=1)
    share_a = mm_left(rows_two, mm(sums, to_two_a))

    for level in (fine, mid, two, three, four):
        level.clear()
    pl.when(has_high)(lambda: z_copy(0).wait_recv())
    pl.when(has_low)(lambda: z_copy(1).wait_recv())
    for k in range(2):
        extended = turned[:, k * bx * by : (k + 1) * bx * by].T
        window[k, pl.ds(at_x, bx), 8 : 8 + by] = extended.reshape(bx, by, 128)

    def faces():
        for ox in offsets_x:
            for oy in (-1, 0, 1):
                if (ox, oy) != (0, 0):
                    yield ox, oy

    def face_copy(ox, oy, arriving):
        target, there = beside(ox, oy, 0)
        home = offsets_x.index(ox) * 3 + 1 + oy
        if ox == 0:
            src_x, dst_x, size_x = at_x, at_x, bx
        elif ox == 2:
            src_x = at_x + (bx - HX) * (1 - me_x)
            dst_x = bx * me_x
            size_x = HX
            if arriving:
                dst_x = bx * (1 - me_x)
        else:
            src_x = at_x + (bx - HX if ox == 1 else 0)
            dst_x = 0 if ox == 1 else HX + bx
            if arriving:
                dst_x = HX + bx if ox == 1 else 0
            size_x = HX
        src_y, size_y = {0: (8, by), 1: (by, 8), -1: (8, 8)}[oy]
        dst_y = {0: 8, 1: 0, -1: 8 + by}[-oy if arriving else oy]
        if arriving:
            recv = home
        else:
            recv = offsets_x.index(ox if ox in (0, 2) else -ox) * 3 + 1 - oy
        return pltpu.make_async_remote_copy(
            src_ref=window.at[:, pl.ds(src_x, size_x), src_y : src_y + size_y],
            dst_ref=window.at[:, pl.ds(dst_x, size_x), dst_y : dst_y + size_y],
            send_sem=w_send.at[home], recv_sem=w_recv.at[recv],
            device_id=target, device_id_type=MESH), there

    for ox, oy in faces():
        copy, there = face_copy(ox, oy, False)
        guarded(there, copy.start)

    zoff = iota((24, 128), 1)
    zoff = jnp.where(zoff < 96, zoff, zoff - 128)
    row = me_y * half_y - half_y + iota((24, 128), 0)
    z_at = me_z * half_z + zoff
    mask_one = jnp.where(
        (row >= 0) & (row < gy * half_y) & (z_at >= 0) & (z_at < gz * half_z) & (zoff < 64), 1.0, 0.0)
    lane_group = lane // 32

    def unpack_one(near, own, dst):
        near[(at_one // half_x) * 9 + 4] = own[...]
        for sx in range(min(gx, 3) if not small_x else gx):
            for sy in range(3):
                for q in range(half_x // 4):
                    base = (sx * 3 + sy) * 3
                    low = pltpu.roll(near[base, q], 96, 1)
                    mine = near[base + 1, q]
                    high = pltpu.roll(near[base + 2, q], 32, 1)
                    for j in range(4):
                        piece = jnp.where(
                            lane_group == j, mine,
                            jnp.where(lane_group == (j + 1) % 4, high,
                                      jnp.where(lane_group == (j + 3) % 4, low, 0.0)))
                        if j:
                            piece = pltpu.roll(piece, 128 - 32 * j, 1)
                        dst[sx * half_x + 4 * q + j, 8 * sy : 8 * sy + 8] = piece

    bricks(own_a, near_a, a_send, a_recv, "recv")
    unpack_one(near_a, own_a, mid.diag)

    zoff0 = iota((by + 16, 128), 1)
    zoff0 = jnp.where(zoff0 < 96, zoff0, zoff0 - 128)
    row0 = me_y * by - 8 + iota((by + 16, 128), 0)
    z0 = me_z * bz + zoff0
    mask_zero = jnp.where(
        (row0 >= 0) & (row0 < gy * by) & (z0 >= 0) & (z0 < gz * bz)
        & (zoff0 < bz + 8) & (zoff0 >= -8), 1.0, 0.0)

    def plane_ok(start, total):
        if small_x:
            return None
        return lambda x: jnp.where((start + x >= 0) & (start + x < total), 1.0, 0.0)

    for ox, oy in faces():
        copy, there = face_copy(ox, oy, True)
        guarded(there, copy.wait_recv)
    fine.init(lambda x: window[0, x], lambda x: window[1, x], mask_zero,
              plane_ok(me_x * bx - HX, gx * bx))
    fine.down()

    pack_one(lambda x: fine.r[at_x + x, 8 : 8 + by], own_f)
    bricks(own_f, near_f, f_send, f_recv, "start")
    bricks(own_f, near_f, f_send, f_recv, "recv")
    unpack_one(near_f, own_f, mid.r)
    mid.init(lambda x: mid.r[x], lambda x: mid.diag[x], mask_one,
             plane_ok(me_x * half_x - half_x, gx * half_x))
    mid.down()

    sums = jnp.concatenate(
        [mid.r[at_one + 2 * i, 8:16] + mid.r[at_one + 2 * i + 1, 8:16] for i in range(4)], axis=1)
    share = mm_left(rows_two, mm(sums, to_two)) + share_a
    pack[...] = share
    gathered[flat_me] = share

    def spread(k, carry):
        pltpu.make_async_remote_copy(
            src_ref=pack, dst_ref=gathered.at[flat_me], send_sem=g_send, recv_sem=g_recv,
            device_id=place(k), device_id_type=MESH).start()
        return carry

    lax.fori_loop(1, devices, spread, 0)
    everything = pltpu.make_async_remote_copy(
        src_ref=gathered.at[0 : devices - 1], dst_ref=gathered.at[0 : devices - 1],
        send_sem=g_send, recv_sem=g_recv, device_id=place(1), device_id_type=MESH)
    everything.wait_recv()

    lane16 = lane // 16

    def unpack_two(sx, carry):
        for pair in range(gy // 2):
            blocks = []
            for sz in range(gz):
                first = (sx * gy + 2 * pair) * gz + sz
                both = jnp.concatenate([gathered[first], gathered[first + gz]], axis=0)
                shift = 16 * (sz % 8)
                blocks.append(pltpu.roll(both, shift, 1) if shift else both)
            for k, dst in enumerate((whole_f, whole_a)):
                for i in range(4):
                    for tile in range((gz + 7) // 8):
                        piece = jnp.zeros((8, 128), F32)
                        for sz in range(8 * tile, min(gz, 8 * tile + 8)):
                            piece = jnp.where(lane16 == (4 * k + i + sz) % 8, blocks[sz], piece)
                        shift = (128 - 16 * (4 * k + i)) % 128
                        if shift:
                            piece = pltpu.roll(piece, shift, 1)
                        dst[4 * sx + i, 8 * pair : 8 * pair + 8, 128 * tile : 128 * tile + 128] = piece
        return carry

    lax.fori_loop(0, gx, unpack_two, 0)

    def whole_mask(level, rows, lanes):
        shape = (level.rows, level.lanes)
        return jnp.where((iota(shape, 0) < rows) & (iota(shape, 1) < lanes), 1.0, 0.0)

    def matrices(above, below):
        shape = (above.lanes, below.lanes)
        narrow = ones_where(iota(shape, 0) // 2 == iota(shape, 1), 0.5)
        shape = (below.rows, above.rows)
        return narrow, ones_where(iota(shape, 1) // 2 == iota(shape, 0))

    def restrict(src, dst, narrow, short):
        for i in range(dst.shape[0]):
            dst[i] = mm_left(short, mm(src[2 * i] + src[2 * i + 1], narrow))

    def prolong(values, dst, wide, tall):
        for i in range(values.shape[0]):
            spread_out = mm_left(tall, mm(values[i], wide))
            dst[2 * i + 1, 8 : 8 + dst.shape[1] - 16] = spread_out
            dst[2 * i + 2, 8 : 8 + dst.shape[1] - 16] = spread_out

    def wide_tall(above, below):
        shape = (below.lanes, above.lanes)
        wide = ones_where(iota(shape, 1) // 2 == iota(shape, 0))
        shape = (above.rows, below.rows)
        return wide, ones_where(iota(shape, 0) // 2 == iota(shape, 1))

    y2, z2 = gy * half_y // 2, gz * half_z // 2
    narrow2, short2 = matrices(two, three)
    narrow3, short3 = matrices(three, four)
    restrict(whole_a, a3, narrow2, short2)
    restrict(a3, a4, narrow3, short3)
    two.init(lambda x: whole_f[x], lambda x: whole_a[x], whole_mask(two, y2, z2), unroll=4)
    two.down(unroll=4)
    restrict(two.r, f3, narrow2, short2)
    three.init(lambda x: f3[x], lambda x: a3[x], whole_mask(three, y2 // 2, z2 // 2), unroll=4)
    three.down(unroll=4)
    restrict(three.r, f4, narrow3, short3)
    four.init(lambda x: f4[x], lambda x: a4[x], whole_mask(four, y2 // 4, z2 // 4))
    four.down(False)
    prolong(four.v, three.d0, *wide_tall(three, four))
    three.up(unroll=4)
    prolong(three.v, two.d0, *wide_tall(two, three))
    two.up(unroll=4)

    shape = (two.lanes, 128)
    zoff1 = iota(shape, 1)
    zoff1 = jnp.where(zoff1 < 96, zoff1, zoff1 - 128)
    coarse_z = (me_z * half_z + zoff1 + 2 * z2) // 2 - z2
    wide = ones_where((iota(shape, 0) == coarse_z) & (iota(shape, 0) < z2))
    shape = (mid.rows, two.rows)
    coarse_y = (me_y * half_y - half_y + iota(shape, 0) + 2 * y2) // 2 - y2
    tall = ones_where(iota(shape, 1) == coarse_y)
    pairs = mid.planes // 2
    for i in range(pairs):
        if small_x:
            values = two.v[i]
        else:
            at = me_x * (half_x // 2) - half_x // 2 + i
            inside = (at >= 0) & (at < two.planes)
            values = two.v[jnp.clip(at, 0, two.planes - 1)] * jnp.where(inside, 1.0, 0.0)
        spread_out = mm_left(tall, mm(values, wide))
        mid.d0[2 * i + 1, 8 : 8 + mid.rows] = spread_out
        mid.d0[2 * i + 2, 8 : 8 + mid.rows] = spread_out
    mid.up()

    shape = (128, 128)
    lane0 = iota(shape, 1)
    from_lane = jnp.where(lane0 < 96, lane0 // 2, 64 + lane0 // 2)
    wide = ones_where((iota(shape, 0) == from_lane) & ((lane0 < bz + 8) | (lane0 >= 120)))
    shape = (fine.rows, mid.rows)
    tall = ones_where(iota(shape, 1) == iota(shape, 0) // 2 + 4)
    at = (bx // 2 - HX // 2) * me_x if small_x else bx // 2 - HX // 2
    for i in range(fine.planes // 2):
        spread_out = mm_left(tall, mm(mid.v[at + i], wide))
        fine.d0[2 * i + 1, 8 : 8 + fine.rows] = spread_out
        fine.d0[2 * i + 2, 8 : 8 + fine.rows] = spread_out
    fine.up(True)
    p_ref[...] = fine.v[pl.ds(at_x, bx), 8 : 8 + by, 0:bz]
    e_ref[...] = fine.r[pl.ds(at_x, bx), 8 : 8 + by, 0:bz]

    pl.when(has_high)(lambda: z_copy(1).wait_send())
    pl.when(has_low)(lambda: z_copy(0).wait_send())
    bricks(own_a, near_a, a_send, a_recv, "send")
    bricks(own_f, near_f, f_send, f_recv, "send")
    for ox, oy in faces():
        copy, there = face_copy(ox, oy, False)
        guarded(there, copy.wait_send)
    everything.wait_send()


def shards(counts, right_side, diagonal):
    gx, gy, gz = counts
    bx, by, bz = right_side.shape
    slots_x = min(gx, 2) if gx <= 2 else 3
    x0 = bx + (HX * (gx - 1) if gx <= 2 else 2 * HX)

    def lanes_for(size):
        return 128 * ((size + 128) // 128)

    def level(planes, rows, lanes):
        plain = pltpu.VMEM((planes, rows, lanes), F32)
        padded = pltpu.VMEM((planes + 2, rows + 16, lanes), F32)
        return [plain] * 4 + [padded] * 2

    two = (gx * bx // 4, gy * by // 4, lanes_for(gz * bz // 4))
    three = (gx * bx // 8, gy * by // 8, lanes_for(gz * bz // 8))
    four = (gx * bx // 16, max(8, gy * by // 16), lanes_for(gz * bz // 16))
    brick = (bx // 8, by // 2, 128)
    near = (slots_x * 9,) + brick
    scratch = [
        pltpu.VMEM((128, 2 * bx * by), F32),
        pltpu.VMEM((2, x0, by + 16, 128), F32),
        pltpu.VMEM(near, F32),
        pltpu.VMEM(near, F32),
        pltpu.VMEM(brick, F32),
        pltpu.VMEM(brick, F32),
        pltpu.VMEM((by // 4, 128), F32),
        pltpu.VMEM((gx * gy * gz, by // 4, 128), F32),
        pltpu.VMEM(two, F32),
        pltpu.VMEM(two, F32),
        pltpu.VMEM(three, F32),
        pltpu.VMEM(three, F32),
        pltpu.VMEM(four, F32),
        pltpu.VMEM(four, F32),
    ]
    scratch += level(x0, by + 16, 128)
    scratch += level(slots_x * bx // 2, 24, 128)
    scratch += level(*two) + level(*three) + level(*four)
    dma = pltpu.SemaphoreType.DMA
    scratch += [dma((2,)), dma((2,))]
    scratch += [dma((slots_x * 3,))] * 2
    scratch += [dma((slots_x * 9,))] * 4
    scratch += [dma, dma]
    out = jax.ShapeDtypeStruct(right_side.shape, F32)
    vmem = pl.BlockSpec(memory_space=pltpu.VMEM)
    return pl.pallas_call(
        functools.partial(kernel, counts),
        out_shape=(out, out),
        in_specs=[vmem, vmem],
        out_specs=(vmem, vmem),
        scratch_shapes=scratch,
        compiler_params=pltpu.CompilerParams(
            collective_id=0, has_side_effects=True, vmem_limit_bytes=56 * 1024 * 1024
        ),
    )(right_side, diagonal)


def solution(mesh):
    spec = P("gx", "gy", "gz")
    counts = tuple(mesh.shape[name] for name in ("gx", "gy", "gz"))
    return jax.shard_map(
        functools.partial(shards, counts), mesh=mesh, in_specs=(spec, spec),
        out_specs=(spec, spec), check_vma=False)
```

```python
import functools
import jax
import jax.numpy as jnp
from jax import lax
from jax.experimental import pallas as pl
from jax.experimental.pallas import tpu as pltpu
from jax.sharding import PartitionSpec as P

CHEB_LOW = 0.3
CHEB_HIGH = 2.0
MIDDLE = 0.5 * (CHEB_HIGH + CHEB_LOW)
HALF = 0.5 * (CHEB_HIGH - CHEB_LOW)
SIGMA = MIDDLE / HALF
Q0 = 1.0 / SIGMA
Q1 = 1.0 / (2.0 * SIGMA - Q0)
Q2 = 1.0 / (2.0 * SIGMA - Q1)
STEP0 = (0.0, 1.0 / MIDDLE)
STEP1 = (Q1 * Q0, 2.0 * Q1 / HALF)
STEP2 = (Q2 * Q1, 2.0 * Q2 / HALF)

MESH = pl.DeviceIdType.MESH
HX = 6
BF = jnp.bfloat16
F32 = jnp.float32


def ones_where(condition, value=1.0):
    return jnp.where(condition, value, 0.0).astype(BF)


def iota(shape, dim):
    return lax.broadcasted_iota(jnp.int32, shape, dim)


def mm(values, matrix):
    rows = values.shape[0]
    high = values.astype(BF).astype(F32)
    both = jnp.concatenate([high, values - high], axis=0).astype(BF)
    out = jnp.dot(both, matrix, preferred_element_type=F32)
    return out[:rows] + out[rows:]


def mm_left(matrix, values):
    lanes = values.shape[1]
    high = values.astype(BF).astype(F32)
    both = jnp.concatenate([high, values - high], axis=1).astype(BF)
    out = jnp.dot(matrix, both, preferred_element_type=F32)
    return out[:, :lanes] + out[:, lanes:]


class Level:
    def __init__(self, refs, halo=0, sides=0, me=0):
        self.r, self.diag, self.inv, self.v, self.d0, self.d1, self.d2 = refs
        self.planes, self.rows, self.lanes = self.r.shape
        self.halo, self.sides, self.me = halo, sides, me
        self.group = max(1, 8 // (self.rows // 8 * (self.lanes // 128)))

    def loop(self, body, halo=0):
        trim = self.halo - halo
        count = self.planes - self.sides * trim
        base = {0: 0, 1: trim * self.me, 2: trim}[self.sides]
        if count <= 32:
            at = 0
            while at < count:
                size = min(self.group, count - at)
                body(base + at, size)
                at += size
            return
        size = next(k for k in (4, 3, 2, 1) if count % k == 0)

        def step(k, carry):
            body(base + k * size, size)
            return carry

        lax.fori_loop(0, count // size, step, 0)

    def clear(self):
        zeros = jnp.zeros(self.d0.shape[1:], F32)
        edge = jnp.zeros(self.d0.shape[:1] + (8,) + self.d0.shape[2:], F32)
        for d in (self.d0, self.d1, self.d2):
            d[0] = zeros
            d[self.planes + 1] = zeros
            d[:, 0:8] = edge
            d[:, 8 + self.rows :] = edge

    def scale(self, added, mask, plane_ok=None):
        def body(x0, size):
            for x in range(size):
                diag = 6.0 + added(x0 + x)
                inv = mask / diag
                if plane_ok is not None:
                    inv = inv * plane_ok(x0 + x)
                self.diag[x0 + x] = diag
                self.inv[x0 + x] = inv

        self.loop(body, self.halo)

    def init(self, source):
        rows = self.rows

        def body(x0, size):
            f = [source(x0 + x) for x in range(size)]
            d = [self.inv[x0 + x] * f[x] * (1.0 / MIDDLE) for x in range(size)]
            for x in range(size):
                self.r[x0 + x] = f[x]
                self.d0[x0 + x + 1, 8 : 8 + rows] = d[x]

        self.loop(body, self.halo)

    def sweep(self, old, new, step, halo):
        rows = self.rows

        def body(x0, size):
            ds = [old[x0 + k, 8 : 8 + rows] for k in range(size + 2)]
            rs, fresh = [], []
            for k in range(size):
                d = ds[k + 1]
                beside = ds[k] + ds[k + 2]
                beside = beside + (old[x0 + k + 1, 7 : 7 + rows] + old[x0 + k + 1, 9 : 9 + rows])
                beside = beside + (pltpu.roll(d, 1, 1) + pltpu.roll(d, self.lanes - 1, 1))
                r = self.r[x0 + k] - self.diag[x0 + k] * d + beside
                rs.append(r)
                if step is not None:
                    keep, gain = step
                    e = gain * (self.inv[x0 + k] * r)
                    fresh.append(keep * d + e if keep else e)
            for k in range(size):
                self.r[x0 + k] = rs[k]
                if step is not None:
                    new[x0 + k + 1, 8 : 8 + rows] = fresh[k]

        self.loop(body, halo)

    def total(self, halo, first):
        rows = self.rows

        def body(x0, size):
            for k in range(size):
                at = (x0 + k + 1, slice(8, 8 + rows))
                sums = self.d0[at] + self.d1[at] + self.d2[at]
                self.v[x0 + k] = sums if first else self.v[x0 + k] + sums

        self.loop(body, halo)

    def total_last(self, halo=0):
        def body(x0, size):
            for k in range(size):
                self.v[x0 + k] = self.v[x0 + k] + self.d0[x0 + k + 1, 8 : 8 + self.rows]

        self.loop(body, halo)

    def down(self, halo=0, want_residual=True):
        step = 1 if self.sides else 0
        self.sweep(self.d0, self.d1, STEP1, halo + 2 * step)
        self.sweep(self.d1, self.d2, STEP2, halo + step)
        if want_residual:
            self.sweep(self.d2, None, None, halo)

    def up(self, halo=0, want_residual=False):
        step = 1 if self.sides else 0
        self.sweep(self.d0, self.d1, STEP0, halo + 2 * step)
        self.sweep(self.d1, self.d2, STEP1, halo + step)
        self.total(halo, False)
        self.sweep(self.d2, self.d0, STEP2, halo)
        if want_residual:
            self.sweep(self.d0, None, None, halo - step)


def kernel(counts, f_ref, a_ref, p_ref, e_ref, turned, window, near_a, near_f, own_a, own_f,
           pack, gathered, whole_f, whole_a, f3, a3, f4, a4, *rest):
    gx, gy, gz = counts
    bx, by, bz = f_ref.shape
    devices = gx * gy * gz
    z_send, z_recv, w_send, w_recv, a_send, a_recv, f_send, f_recv, g_send, g_recv = rest[35:]
    me_x = lax.axis_index("gx")
    me_y = lax.axis_index("gy")
    me_z = lax.axis_index("gz")
    small_x = gx <= 2
    sides = gx - 1 if small_x else 2
    fine = Level(rest[0:7], HX, sides, me_x)
    mid = Level(rest[7:14], bx // 2, sides, me_x)
    two, three, four = [Level(rest[7 * k : 7 * k + 7]) for k in (2, 3, 4)]
    at_x = HX * me_x if small_x else HX
    at_one = (bx // 2) * me_x if small_x else bx // 2
    half_x, half_y, half_z = bx // 2, by // 2, bz // 2

    turned[...] = jnp.zeros_like(turned)
    padding = jnp.zeros((bx * by, 128 - bz), F32)
    for k, ref in enumerate((f_ref, a_ref)):
        flat = jnp.concatenate([ref[...].reshape(bx * by, bz), padding], axis=1)
        turned[0:bz, k * bx * by : (k + 1) * bx * by] = flat.T[0:bz]
    for ref in (near_a, near_f, whole_f, whole_a, f4, a4):
        ref[...] = jnp.zeros_like(ref)

    def clear_window(x, carry):
        window[0, x] = jnp.zeros(window.shape[2:], F32)
        window[1, x] = jnp.zeros(window.shape[2:], F32)
        return carry

    lax.fori_loop(0, window.shape[1], clear_window, 0)

    barrier = pltpu.get_barrier_semaphore()
    flat_me = (me_x * gy + me_y) * gz + me_z

    def place(k):
        other = lax.rem(flat_me + k, devices)
        return (lax.div(other, gy * gz), lax.rem(lax.div(other, gz), gy), lax.rem(other, gz))

    def greet(k, carry):
        pl.semaphore_signal(barrier, inc=1, device_id=place(k), device_id_type=MESH)
        return carry

    lax.fori_loop(1, devices, greet, 0)
    pl.semaphore_wait(barrier, devices - 1)

    def z_copy(way):
        src = turned.at[bz - 8 : bz] if way else turned.at[0:8]
        dst = turned.at[120:128] if way else turned.at[bz : bz + 8]
        return pltpu.make_async_remote_copy(
            src_ref=src, dst_ref=dst, send_sem=z_send.at[way], recv_sem=z_recv.at[way],
            device_id=(me_x, me_y, me_z + (1 if way else -1)), device_id_type=MESH)

    has_low, has_high = me_z > 0, me_z < gz - 1
    pl.when(has_high)(lambda: z_copy(1).start())
    pl.when(has_low)(lambda: z_copy(0).start())

    inner = iota((128, 128), 0)
    column = iota((128, 128), 1)

    def packing(width, kept, start):
        return jnp.concatenate(
            [ones_where((column == start + width * j + (inner >> 1)) & (inner < kept), 0.5)
             for j in range(4)], axis=0)

    def halved(ref, x, start, count):
        sums = None
        for plane in (x, x + 1):
            for odd in (0, 1):
                term = ref[plane, pl.ds(start + odd, count, 2)]
                sums = term if sums is None else sums + term
        return sums

    to_one = packing(32, bz, 0)

    def pack_one(ref, first, start, out):
        quads = []
        for q in range(half_x // 4):
            planes = [halved(ref, first + 2 * (4 * q + j), start, half_y) for j in range(4)]
            if planes[0].shape[1] < 128:
                pad = jnp.zeros((half_y, 128 - planes[0].shape[1]), F32)
                planes = [jnp.concatenate([plane, pad], axis=1) for plane in planes]
            quads.append(jnp.concatenate(planes, axis=1))
        packed = mm(jnp.concatenate(quads, axis=0), to_one)
        for q in range(half_x // 4):
            out[q] = packed[q * half_y : (q + 1) * half_y]

    pack_one(a_ref, 0, 0, own_a)

    offsets_x = (0,) if gx == 1 else ((0, 2) if gx == 2 else (-1, 0, 1))

    def around():
        for ox in offsets_x:
            for oy in (-1, 0, 1):
                for oz in (-1, 0, 1):
                    if (ox, oy, oz) != (0, 0, 0):
                        yield ox, oy, oz

    def beside(ox, oy, oz):
        tx = me_x if ox == 0 else (1 - me_x if ox == 2 else me_x + ox)
        ty, tz = me_y + oy, me_z + oz
        there = None
        tests = []
        if abs(ox) == 1:
            tests.append((tx >= 0) & (tx < gx))
        if oy:
            tests.append(ty >= 0 if oy < 0 else ty < gy)
        if oz:
            tests.append(tz >= 0 if oz < 0 else tz < gz)
        for test in tests:
            there = test if there is None else there & test
        return (tx, ty, tz), there

    def guarded(there, act):
        if there is None:
            act()
        else:
            pl.when(there)(act)

    def brick_copy(offset, own, near, send, recv, arriving):
        ox, oy, oz = offset
        target, there = beside(ox, oy, oz)
        if arriving:
            slot_x = target[0] if small_x else 1 + ox
            slot = (slot_x * 3 + 1 + oy) * 3 + 1 + oz
        else:
            slot_x = me_x if small_x else 1 - ox
            slot = (slot_x * 3 + 1 - oy) * 3 + 1 - oz
        home = ((offsets_x.index(ox)) * 3 + 1 + oy) * 3 + 1 + oz
        copy = pltpu.make_async_remote_copy(
            src_ref=own, dst_ref=near.at[slot], send_sem=send.at[home], recv_sem=recv.at[slot],
            device_id=target, device_id_type=MESH)
        return copy, there

    def bricks(own, near, send, recv, what):
        for offset in around():
            copy, there = brick_copy(offset, own, near, send, recv, what == "recv")
            act = {"start": copy.start, "recv": copy.wait_recv, "send": copy.wait_send}[what]
            guarded(there, act)

    bricks(own_a, near_a, a_send, a_recv, "start")

    to_two = packing(16, half_z, 0)
    to_two_a = packing(16, half_z, 64)
    rows_two = ones_where((iota((half_y // 2, half_y), 1) >> 1) == iota((half_y // 2, half_y), 0))
    lane = iota((8, 128), 1)

    def brick_plane(own, x):
        moved = own[x // 4]
        if x % 4:
            moved = pltpu.roll(moved, 128 - 32 * (x % 4), 1)
        return moved

    sums = jnp.concatenate(
        [brick_plane(own_a, 2 * i) + brick_plane(own_a, 2 * i + 1) for i in range(4)], axis=1)
    share_a = mm_left(rows_two, mm(sums, to_two_a))

    for level in (fine, mid, two, three, four):
        level.clear()
    pl.when(has_high)(lambda: z_copy(0).wait_recv())
    pl.when(has_low)(lambda: z_copy(1).wait_recv())
    for k in range(2):
        extended = turned[:, k * bx * by : (k + 1) * bx * by].T
        window[k, pl.ds(at_x, bx), 8 : 8 + by] = extended.reshape(bx, by, 128)

    def faces():
        for ox in offsets_x:
            for oy in (-1, 0, 1):
                if (ox, oy) != (0, 0):
                    yield ox, oy

    def face_copy(ox, oy, arriving):
        target, there = beside(ox, oy, 0)
        home = offsets_x.index(ox) * 3 + 1 + oy
        if ox == 0:
            src_x, dst_x, size_x = at_x, at_x, bx
        elif ox == 2:
            src_x = at_x + (bx - HX) * (1 - me_x)
            dst_x = bx * me_x
            size_x = HX
            if arriving:
                dst_x = bx * (1 - me_x)
        else:
            src_x = at_x + (bx - HX if ox == 1 else 0)
            dst_x = 0 if ox == 1 else HX + bx
            if arriving:
                dst_x = HX + bx if ox == 1 else 0
            size_x = HX
        src_y, size_y = {0: (8, by), 1: (by, 8), -1: (8, 8)}[oy]
        dst_y = {0: 8, 1: 0, -1: 8 + by}[-oy if arriving else oy]
        if arriving:
            recv = home
        else:
            recv = offsets_x.index(ox if ox in (0, 2) else -ox) * 3 + 1 - oy
        return pltpu.make_async_remote_copy(
            src_ref=window.at[:, pl.ds(src_x, size_x), src_y : src_y + size_y],
            dst_ref=window.at[:, pl.ds(dst_x, size_x), dst_y : dst_y + size_y],
            send_sem=w_send.at[home], recv_sem=w_recv.at[recv],
            device_id=target, device_id_type=MESH), there

    for ox, oy in faces():
        copy, there = face_copy(ox, oy, False)
        guarded(there, copy.start)

    zoff = iota((24, 128), 1)
    zoff = jnp.where(zoff < 96, zoff, zoff - 128)
    row = me_y * half_y - half_y + iota((24, 128), 0)
    z_at = me_z * half_z + zoff
    mask_one = jnp.where(
        (row >= 0) & (row < gy * half_y) & (z_at >= 0) & (z_at < gz * half_z) & (zoff < 64), 1.0, 0.0)
    lane_group = lane >> 5

    def unpack_one(near, own, dst):
        near[(at_one // half_x) * 9 + 4] = own[...]
        for sx in range(min(gx, 3) if not small_x else gx):
            for sy in range(3):
                for q in range(half_x // 4):
                    base = (sx * 3 + sy) * 3
                    low = pltpu.roll(near[base, q], 96, 1)
                    mine = near[base + 1, q]
                    high = pltpu.roll(near[base + 2, q], 32, 1)
                    for j in range(4):
                        piece = jnp.where(
                            lane_group == j, mine,
                            jnp.where(lane_group == (j + 1) % 4, high,
                                      jnp.where(lane_group == (j + 3) % 4, low, 0.0)))
                        if j:
                            piece = pltpu.roll(piece, 128 - 32 * j, 1)
                        dst[sx * half_x + 4 * q + j, 8 * sy : 8 * sy + 8] = piece

    bricks(own_a, near_a, a_send, a_recv, "recv")
    unpack_one(near_a, own_a, mid.diag)

    def plane_ok(start, total):
        if small_x:
            return None
        return lambda x: jnp.where((start + x >= 0) & (start + x < total), 1.0, 0.0)

    mid.scale(lambda x: mid.diag[x], mask_one, plane_ok(me_x * half_x - half_x, gx * half_x))

    zoff0 = iota((by + 16, 128), 1)
    zoff0 = jnp.where(zoff0 < 96, zoff0, zoff0 - 128)
    row0 = me_y * by - 8 + iota((by + 16, 128), 0)
    z0 = me_z * bz + zoff0
    mask_zero = jnp.where(
        (row0 >= 0) & (row0 < gy * by) & (z0 >= 0) & (z0 < gz * bz)
        & (zoff0 < bz + 8) & (zoff0 >= -8), 1.0, 0.0)

    for ox, oy in faces():
        copy, there = face_copy(ox, oy, True)
        guarded(there, copy.wait_recv)
    fine.scale(lambda x: window[1, x], mask_zero, plane_ok(me_x * bx - HX, gx * bx))
    fine.init(lambda x: window[0, x])
    fine.down(3)

    pack_one(fine.r, at_x, 8, own_f)
    bricks(own_f, near_f, f_send, f_recv, "start")
    fine.total(0, True)
    bricks(own_f, near_f, f_send, f_recv, "recv")
    unpack_one(near_f, own_f, mid.r)
    mid.init(lambda x: mid.r[x])
    mid.down(4)

    sums = jnp.concatenate([halved(mid.r, at_one + 2 * i, 8, half_y // 2) for i in range(4)], axis=1)
    share = mm(sums, to_two) + share_a
    pack[...] = share
    gathered[flat_me] = share

    def spread(k, carry):
        pltpu.make_async_remote_copy(
            src_ref=pack, dst_ref=gathered.at[flat_me], send_sem=g_send, recv_sem=g_recv,
            device_id=place(k), device_id_type=MESH).start()
        return carry

    lax.fori_loop(1, devices, spread, 0)
    mid.total(2, True)
    everything = pltpu.make_async_remote_copy(
        src_ref=gathered.at[0 : devices - 1], dst_ref=gathered.at[0 : devices - 1],
        send_sem=g_send, recv_sem=g_recv, device_id=place(1), device_id_type=MESH)
    everything.wait_recv()

    lane16 = lane >> 4

    def unpack_two(sx, carry):
        for pair in range(gy // 2):
            blocks = []
            for sz in range(gz):
                first = (sx * gy + 2 * pair) * gz + sz
                both = jnp.concatenate([gathered[first], gathered[first + gz]], axis=0)
                shift = 16 * (sz % 8)
                blocks.append(pltpu.roll(both, shift, 1) if shift else both)
            for k, dst in enumerate((whole_f, whole_a)):
                for i in range(4):
                    for tile in range((gz + 7) // 8):
                        piece = jnp.zeros((8, 128), F32)
                        for sz in range(8 * tile, min(gz, 8 * tile + 8)):
                            piece = jnp.where(lane16 == (4 * k + i + sz) % 8, blocks[sz], piece)
                        shift = (128 - 16 * (4 * k + i)) % 128
                        if shift:
                            piece = pltpu.roll(piece, shift, 1)
                        dst[4 * sx + i, 8 * pair : 8 * pair + 8, 128 * tile : 128 * tile + 128] = piece
        return carry

    lax.fori_loop(0, gx, unpack_two, 0)

    def whole_mask(level, rows, lanes):
        shape = (level.rows, level.lanes)
        return jnp.where((iota(shape, 0) < rows) & (iota(shape, 1) < lanes), 1.0, 0.0)

    def restrict(src, dst):
        planes, lanes = dst.shape[0], src.shape[2]
        shape = (lanes, dst.shape[2])
        narrow = ones_where((iota(shape, 0) >> 1) == iota(shape, 1), 0.5)
        sums = [src[2 * i] + src[2 * i + 1] for i in range(planes)]
        out = mm(jnp.concatenate(sums, axis=0), narrow)
        shape = (dst.shape[1], src.shape[1])
        fold = ones_where((iota(shape, 1) >> 1) == iota(shape, 0))
        size = src.shape[1]
        beside_each_other = jnp.concatenate(
            [out[i * size : (i + 1) * size] for i in range(planes)], axis=1)
        out = mm_left(fold, beside_each_other)
        for i in range(planes):
            dst[i] = out[:, i * dst.shape[2] : (i + 1) * dst.shape[2]]

    def prolong(values, rows, wide, dst):
        out = mm(jnp.concatenate(values, axis=0), wide)
        if dst.shape[2] != 128:
            shape = (2 * rows, rows)
            tall = ones_where((iota(shape, 0) >> 1) == iota(shape, 1))
            for i in range(len(values)):
                doubled = mm_left(tall, out[i * rows : (i + 1) * rows])
                for plane in (2 * i + 1, 2 * i + 2):
                    dst[plane, 8 : 8 + 2 * rows] = doubled
            return
        for i in range(len(values)):
            for plane in (2 * i + 1, 2 * i + 2):
                for odd in (0, 1):
                    dst[plane, pl.ds(8 + odd, rows, 2)] = out[i * rows : (i + 1) * rows]

    def widening(above, below):
        shape = (below.lanes, above.lanes)
        return ones_where((iota(shape, 1) >> 1) == iota(shape, 0))

    y2, z2 = gy * half_y // 2, gz * half_z // 2
    restrict(whole_a, a3)
    restrict(a3, a4)
    two.scale(lambda x: whole_a[x], whole_mask(two, y2, z2))
    three.scale(lambda x: a3[x], whole_mask(three, y2 // 2, z2 // 2))
    four.scale(lambda x: a4[x], whole_mask(four, y2 // 4, z2 // 4))
    two.init(lambda x: whole_f[x])
    two.down()
    two.total(0, True)
    restrict(two.r, f3)
    three.init(lambda x: f3[x])
    three.down()
    three.total(0, True)
    restrict(three.r, f4)
    four.init(lambda x: f4[x])
    four.down(0, False)
    four.total(0, True)
    prolong([four.v[i, 0 : three.rows // 2] for i in range(four.planes)], three.rows // 2,
            widening(three, four), three.d0)
    three.up()
    three.total_last()
    prolong([three.v[i] for i in range(three.planes)], three.rows, widening(two, three), two.d0)
    two.up()
    two.total_last()

    shape = (two.lanes, 128)
    zoff1 = iota(shape, 1)
    zoff1 = jnp.where(zoff1 < 96, zoff1, zoff1 - 128)
    coarse_z = (me_z * half_z + zoff1) >> 1
    wide = ones_where((iota(shape, 0) == coarse_z) & (iota(shape, 0) < z2))
    shape = (mid.rows, two.rows)
    coarse_y = (me_y * half_y - half_y + iota(shape, 0)) >> 1
    tall = ones_where(iota(shape, 1) == coarse_y)
    values = []
    for i in range(mid.planes // 2):
        if small_x:
            values.append(two.v[i])
        else:
            at = me_x * (half_x // 2) - half_x // 2 + i
            inside = (at >= 0) & (at < two.planes)
            values.append(two.v[jnp.clip(at, 0, two.planes - 1)] * jnp.where(inside, 1.0, 0.0))
    out = mm(jnp.concatenate(values, axis=0), wide)
    size = two.rows
    out = mm_left(tall, jnp.concatenate(
        [out[i * size : (i + 1) * size] for i in range(len(values))], axis=1))
    for i in range(len(values)):
        spread_out = out[:, 128 * i : 128 * i + 128]
        mid.d0[2 * i + 1, 8 : 8 + mid.rows] = spread_out
        mid.d0[2 * i + 2, 8 : 8 + mid.rows] = spread_out
    mid.up(2)
    mid.total_last(2)

    shape = (128, 128)
    lane0 = iota(shape, 1)
    from_lane = jnp.where(lane0 < 96, lane0 >> 1, 64 + (lane0 >> 1))
    wide = ones_where((iota(shape, 0) == from_lane) & ((lane0 < bz + 8) | (lane0 >= 120)))
    at = (bx // 2 - HX // 2) * me_x if small_x else bx // 2 - HX // 2
    rows = fine.rows // 2
    prolong([mid.v[at + i, 4 : 4 + rows] for i in range(fine.planes // 2)], rows, wide, fine.d0)
    fine.up(1, True)
    p_ref[...] = (fine.v[pl.ds(at_x, bx), 8 : 8 + by]
                  + fine.d0[pl.ds(at_x + 1, bx), 16 : 16 + by])[:, :, 0:bz]
    e_ref[...] = fine.r[pl.ds(at_x, bx), 8 : 8 + by, 0:bz]

    pl.when(has_high)(lambda: z_copy(1).wait_send())
    pl.when(has_low)(lambda: z_copy(0).wait_send())
    bricks(own_a, near_a, a_send, a_recv, "send")
    bricks(own_f, near_f, f_send, f_recv, "send")
    for ox, oy in faces():
        copy, there = face_copy(ox, oy, False)
        guarded(there, copy.wait_send)
    everything.wait_send()


def shards(counts, right_side, diagonal):
    gx, gy, gz = counts
    bx, by, bz = right_side.shape
    slots_x = min(gx, 2) if gx <= 2 else 3
    x0 = bx + (HX * (gx - 1) if gx <= 2 else 2 * HX)

    def lanes_for(size):
        return 128 * ((size + 128) // 128)

    def level(planes, rows, lanes):
        plain = pltpu.VMEM((planes, rows, lanes), F32)
        padded = pltpu.VMEM((planes + 2, rows + 16, lanes), F32)
        return [plain] * 4 + [padded] * 3

    two = (gx * bx // 4, gy * by // 4, lanes_for(gz * bz // 4))
    three = (gx * bx // 8, gy * by // 8, lanes_for(gz * bz // 8))
    four = (gx * bx // 16, max(8, gy * by // 16), lanes_for(gz * bz // 16))
    brick = (bx // 8, by // 2, 128)
    near = (slots_x * 9,) + brick
    scratch = [
        pltpu.VMEM((128, 2 * bx * by), F32),
        pltpu.VMEM((2, x0, by + 16, 128), F32),
        pltpu.VMEM(near, F32),
        pltpu.VMEM(near, F32),
        pltpu.VMEM(brick, F32),
        pltpu.VMEM(brick, F32),
        pltpu.VMEM((by // 4, 128), F32),
        pltpu.VMEM((gx * gy * gz, by // 4, 128), F32),
        pltpu.VMEM(two, F32),
        pltpu.VMEM(two, F32),
        pltpu.VMEM(three, F32),
        pltpu.VMEM(three, F32),
        pltpu.VMEM(four, F32),
        pltpu.VMEM(four, F32),
    ]
    scratch += level(x0, by + 16, 128)
    scratch += level(slots_x * bx // 2, 24, 128)
    scratch += level(*two) + level(*three) + level(*four)
    dma = pltpu.SemaphoreType.DMA
    scratch += [dma((2,)), dma((2,))]
    scratch += [dma((slots_x * 3,))] * 2
    scratch += [dma((slots_x * 9,))] * 4
    scratch += [dma, dma]
    out = jax.ShapeDtypeStruct(right_side.shape, F32)
    vmem = pl.BlockSpec(memory_space=pltpu.VMEM)
    return pl.pallas_call(
        functools.partial(kernel, counts),
        out_shape=(out, out),
        in_specs=[vmem, vmem],
        out_specs=(vmem, vmem),
        scratch_shapes=scratch,
        compiler_params=pltpu.CompilerParams(
            collective_id=0, has_side_effects=True, vmem_limit_bytes=56 * 1024 * 1024
        ),
    )(right_side, diagonal)


def solution(mesh):
    spec = P("gx", "gy", "gz")
    counts = tuple(mesh.shape[name] for name in ("gx", "gy", "gz"))
    return jax.shard_map(
        functools.partial(shards, counts), mesh=mesh, in_specs=(spec, spec),
        out_specs=(spec, spec), check_vma=False)
```

```python
import functools
import jax
import jax.numpy as jnp
from jax import lax
from jax.experimental import pallas as pl
from jax.experimental.pallas import tpu as pltpu
from jax.sharding import PartitionSpec as P

CHEB_LOW = 0.3
CHEB_HIGH = 2.0
MIDDLE = 0.5 * (CHEB_HIGH + CHEB_LOW)
HALF = 0.5 * (CHEB_HIGH - CHEB_LOW)
SIGMA = MIDDLE / HALF
Q0 = 1.0 / SIGMA
Q1 = 1.0 / (2.0 * SIGMA - Q0)
Q2 = 1.0 / (2.0 * SIGMA - Q1)
STEP0 = (0.0, 1.0 / MIDDLE)
STEP1 = (Q1 * Q0, 2.0 * Q1 / HALF)
STEP2 = (Q2 * Q1, 2.0 * Q2 / HALF)

MESH = pl.DeviceIdType.MESH
HX = 6
BF = jnp.bfloat16
F32 = jnp.float32


def ones_where(condition, value=1.0):
    return jnp.where(condition, value, 0.0).astype(BF)


def iota(shape, dim):
    return lax.broadcasted_iota(jnp.int32, shape, dim)


def mm(values, matrix):
    rows = values.shape[0]
    high = values.astype(BF).astype(F32)
    both = jnp.concatenate([high, values - high], axis=0).astype(BF)
    out = jnp.dot(both, matrix, preferred_element_type=F32)
    return out[:rows] + out[rows:]


def mm_left(matrix, values):
    lanes = values.shape[1]
    high = values.astype(BF).astype(F32)
    both = jnp.concatenate([high, values - high], axis=1).astype(BF)
    out = jnp.dot(matrix, both, preferred_element_type=F32)
    return out[:, :lanes] + out[:, lanes:]


class Level:
    def __init__(self, refs, halo=0, sides=0, me=0):
        self.r, self.diag, self.inv, self.v, self.d0, self.d1, self.d2 = refs
        self.planes, self.rows, self.lanes = self.r.shape
        self.halo, self.sides, self.me = halo, sides, me
        self.group = max(1, 8 // (self.rows // 8 * (self.lanes // 128)))

    def loop(self, body, halo=0):
        trim = self.halo - halo
        count = self.planes - self.sides * trim
        base = {0: 0, 1: trim * self.me, 2: trim}[self.sides]
        if count <= 32:
            at = 0
            while at < count:
                size = min(self.group, count - at)
                body(base + at, size)
                at += size
            return
        size = next(k for k in (4, 3, 2, 1) if count % k == 0)

        def step(k, carry):
            body(base + k * size, size)
            return carry

        lax.fori_loop(0, count // size, step, 0)

    def clear(self):
        zeros = jnp.zeros(self.d0.shape[1:], F32)
        edge = jnp.zeros(self.d0.shape[:1] + (8,) + self.d0.shape[2:], F32)
        for d in (self.d0, self.d1, self.d2):
            d[0] = zeros
            d[self.planes + 1] = zeros
            d[:, 0:8] = edge
            d[:, 8 + self.rows :] = edge

    def scale(self, added, mask, plane_ok=None):
        def body(x0, size):
            for x in range(size):
                diag = 6.0 + added(x0 + x)
                inv = mask / diag
                if plane_ok is not None:
                    inv = inv * plane_ok(x0 + x)
                self.diag[x0 + x] = diag
                self.inv[x0 + x] = inv

        self.loop(body, self.halo)

    def init(self, source):
        rows = self.rows

        def body(x0, size):
            f = [source(x0 + x) for x in range(size)]
            d = [self.inv[x0 + x] * f[x] * (1.0 / MIDDLE) for x in range(size)]
            for x in range(size):
                self.r[x0 + x] = f[x]
                self.d0[x0 + x + 1, 8 : 8 + rows] = d[x]

        self.loop(body, self.halo)

    def sweep(self, old, new, step, halo):
        rows = self.rows

        def body(x0, size):
            ds = [old[x0 + k, 8 : 8 + rows] for k in range(size + 2)]
            rs, fresh = [], []
            for k in range(size):
                d = ds[k + 1]
                beside = ds[k] + ds[k + 2]
                beside = beside + (old[x0 + k + 1, 7 : 7 + rows] + old[x0 + k + 1, 9 : 9 + rows])
                beside = beside + (pltpu.roll(d, 1, 1) + pltpu.roll(d, self.lanes - 1, 1))
                r = self.r[x0 + k] - self.diag[x0 + k] * d + beside
                rs.append(r)
                if step is not None:
                    keep, gain = step
                    e = gain * (self.inv[x0 + k] * r)
                    fresh.append(keep * d + e if keep else e)
            for k in range(size):
                self.r[x0 + k] = rs[k]
                if step is not None:
                    new[x0 + k + 1, 8 : 8 + rows] = fresh[k]

        self.loop(body, halo)

    def total(self, halo, first):
        rows = self.rows

        def body(x0, size):
            for k in range(size):
                at = (x0 + k + 1, slice(8, 8 + rows))
                sums = self.d0[at] + self.d1[at] + self.d2[at]
                self.v[x0 + k] = sums if first else self.v[x0 + k] + sums

        self.loop(body, halo)

    def total_last(self, halo=0):
        def body(x0, size):
            for k in range(size):
                self.v[x0 + k] = self.v[x0 + k] + self.d0[x0 + k + 1, 8 : 8 + self.rows]

        self.loop(body, halo)

    def down(self, halo=0, want_residual=True):
        step = 1 if self.sides else 0
        self.sweep(self.d0, self.d1, STEP1, halo + 2 * step)
        self.sweep(self.d1, self.d2, STEP2, halo + step)
        if want_residual:
            self.sweep(self.d2, None, None, halo)

    def up(self, halo=0, want_residual=False):
        step = 1 if self.sides else 0
        self.sweep(self.d0, self.d1, STEP0, halo + 2 * step)
        self.sweep(self.d1, self.d2, STEP1, halo + step)
        self.total(halo, False)
        self.sweep(self.d2, self.d0, STEP2, halo)
        if want_residual:
            self.sweep(self.d0, None, None, halo - step)


def kernel(counts, f_ref, a_ref, p_ref, e_ref, turned, window, near_a, near_f, own_a, own_f,
           pack, gathered, pack_a, gathered_a, whole_f, whole_a, f3, a3, f4, a4, *rest):
    gx, gy, gz = counts
    bx, by, bz = f_ref.shape
    devices = gx * gy * gz
    z_send, z_recv, w_send, w_recv, a_send, a_recv, f_send, f_recv, g_send, g_recv, h_send, h_recv = (
        rest[35:])
    me_x = lax.axis_index("gx")
    me_y = lax.axis_index("gy")
    me_z = lax.axis_index("gz")
    small_x = gx <= 2
    sides = gx - 1 if small_x else 2
    fine = Level(rest[0:7], HX, sides, me_x)
    mid = Level(rest[7:14], bx // 2, sides, me_x)
    two, three, four = [Level(rest[7 * k : 7 * k + 7]) for k in (2, 3, 4)]
    at_x = HX * me_x if small_x else HX
    at_one = (bx // 2) * me_x if small_x else bx // 2
    half_x, half_y, half_z = bx // 2, by // 2, bz // 2

    turned[...] = jnp.zeros_like(turned)
    for ref in (near_a, near_f):
        ref[...] = jnp.zeros_like(ref)

    def clear_window(x, carry):
        window[0, x] = jnp.zeros(window.shape[2:], F32)
        window[1, x] = jnp.zeros(window.shape[2:], F32)
        return carry

    lax.fori_loop(0, window.shape[1], clear_window, 0)

    barrier = pltpu.get_barrier_semaphore()
    flat_me = (me_x * gy + me_y) * gz + me_z

    def place(k):
        other = lax.rem(flat_me + k, devices)
        return (lax.div(other, gy * gz), lax.rem(lax.div(other, gz), gy), lax.rem(other, gz))

    def greet(k, carry):
        pl.semaphore_signal(barrier, inc=1, device_id=place(k), device_id_type=MESH)
        return carry

    lax.fori_loop(1, devices, greet, 0)
    padding = jnp.zeros((bx * by, 128 - bz), F32)
    for k, ref in enumerate((f_ref, a_ref)):
        flat = jnp.concatenate([ref[...].reshape(bx * by, bz), padding], axis=1)
        turned[0:bz, k * bx * by : (k + 1) * bx * by] = flat.T[0:bz]
    for ref in (whole_f, whole_a, f4, a4):
        ref[...] = jnp.zeros_like(ref)
    pl.semaphore_wait(barrier, devices - 1)

    def z_copy(way):
        src = turned.at[bz - 8 : bz] if way else turned.at[0:8]
        dst = turned.at[120:128] if way else turned.at[bz : bz + 8]
        return pltpu.make_async_remote_copy(
            src_ref=src, dst_ref=dst, send_sem=z_send.at[way], recv_sem=z_recv.at[way],
            device_id=(me_x, me_y, me_z + (1 if way else -1)), device_id_type=MESH)

    has_low, has_high = me_z > 0, me_z < gz - 1
    pl.when(has_high)(lambda: z_copy(1).start())
    pl.when(has_low)(lambda: z_copy(0).start())

    inner = iota((128, 128), 0)
    column = iota((128, 128), 1)

    def packing(width, kept, start):
        return jnp.concatenate(
            [ones_where((column == start + width * j + (inner >> 1)) & (inner < kept), 0.5)
             for j in range(4)], axis=0)

    def halved(ref, x, start, count):
        sums = None
        for plane in (x, x + 1):
            for odd in (0, 1):
                term = ref[plane, pl.ds(start + odd, count, 2)]
                sums = term if sums is None else sums + term
        return sums

    to_one = packing(32, bz, 0)

    def pack_one(ref, first, start, out):
        quads = []
        for q in range(half_x // 4):
            planes = [halved(ref, first + 2 * (4 * q + j), start, half_y) for j in range(4)]
            if planes[0].shape[1] < 128:
                pad = jnp.zeros((half_y, 128 - planes[0].shape[1]), F32)
                planes = [jnp.concatenate([plane, pad], axis=1) for plane in planes]
            quads.append(jnp.concatenate(planes, axis=1))
        packed = mm(jnp.concatenate(quads, axis=0), to_one)
        for q in range(half_x // 4):
            out[q] = packed[q * half_y : (q + 1) * half_y]

    pack_one(a_ref, 0, 0, own_a)

    offsets_x = (0,) if gx == 1 else ((0, 2) if gx == 2 else (-1, 0, 1))

    def around():
        for ox in offsets_x:
            for oy in (-1, 0, 1):
                for oz in (-1, 0, 1):
                    if (ox, oy, oz) != (0, 0, 0):
                        yield ox, oy, oz

    def beside(ox, oy, oz):
        tx = me_x if ox == 0 else (1 - me_x if ox == 2 else me_x + ox)
        ty, tz = me_y + oy, me_z + oz
        there = None
        tests = []
        if abs(ox) == 1:
            tests.append((tx >= 0) & (tx < gx))
        if oy:
            tests.append(ty >= 0 if oy < 0 else ty < gy)
        if oz:
            tests.append(tz >= 0 if oz < 0 else tz < gz)
        for test in tests:
            there = test if there is None else there & test
        return (tx, ty, tz), there

    def guarded(there, act):
        if there is None:
            act()
        else:
            pl.when(there)(act)

    def brick_copy(offset, own, near, send, recv, arriving):
        ox, oy, oz = offset
        target, there = beside(ox, oy, oz)
        if arriving:
            slot_x = target[0] if small_x else 1 + ox
            slot = (slot_x * 3 + 1 + oy) * 3 + 1 + oz
        else:
            slot_x = me_x if small_x else 1 - ox
            slot = (slot_x * 3 + 1 - oy) * 3 + 1 - oz
        home = ((offsets_x.index(ox)) * 3 + 1 + oy) * 3 + 1 + oz
        copy = pltpu.make_async_remote_copy(
            src_ref=own, dst_ref=near.at[slot], send_sem=send.at[home], recv_sem=recv.at[slot],
            device_id=target, device_id_type=MESH)
        return copy, there

    def bricks(own, near, send, recv, what):
        for offset in around():
            copy, there = brick_copy(offset, own, near, send, recv, what == "recv")
            act = {"start": copy.start, "recv": copy.wait_recv, "send": copy.wait_send}[what]
            guarded(there, act)

    bricks(own_a, near_a, a_send, a_recv, "start")

    to_two = packing(16, half_z, 0)
    rows_two = ones_where((iota((half_y // 2, half_y), 1) >> 1) == iota((half_y // 2, half_y), 0))
    lane = iota((8, 128), 1)

    def brick_plane(own, x):
        moved = own[x // 4]
        if x % 4:
            moved = pltpu.roll(moved, 128 - 32 * (x % 4), 1)
        return moved

    sums = jnp.concatenate(
        [brick_plane(own_a, 2 * i) + brick_plane(own_a, 2 * i + 1) for i in range(4)], axis=1)
    share_a = mm_left(rows_two, mm(sums, to_two))
    pack_a[...] = share_a
    gathered_a[flat_me] = share_a

    def spread(src, dst, send, recv):
        def one(k, carry):
            pltpu.make_async_remote_copy(
                src_ref=src, dst_ref=dst.at[flat_me], send_sem=send, recv_sem=recv,
                device_id=place(k), device_id_type=MESH).start()
            return carry

        lax.fori_loop(1, devices, one, 0)
        return pltpu.make_async_remote_copy(
            src_ref=dst.at[0 : devices - 1], dst_ref=dst.at[0 : devices - 1],
            send_sem=send, recv_sem=recv, device_id=place(1), device_id_type=MESH)


    everything_a = spread(pack_a, gathered_a, h_send, h_recv)

    for level in (fine, mid, two, three, four):
        level.clear()
    pl.when(has_high)(lambda: z_copy(0).wait_recv())
    pl.when(has_low)(lambda: z_copy(1).wait_recv())
    for k in range(2):
        extended = turned[:, k * bx * by : (k + 1) * bx * by].T
        window[k, pl.ds(at_x, bx), 8 : 8 + by] = extended.reshape(bx, by, 128)

    def faces():
        for ox in offsets_x:
            for oy in (-1, 0, 1):
                if (ox, oy) != (0, 0):
                    yield ox, oy

    def face_copy(ox, oy, arriving):
        target, there = beside(ox, oy, 0)
        home = offsets_x.index(ox) * 3 + 1 + oy
        if ox == 0:
            src_x, dst_x, size_x = at_x, at_x, bx
        elif ox == 2:
            src_x = at_x + (bx - HX) * (1 - me_x)
            dst_x = bx * me_x
            size_x = HX
            if arriving:
                dst_x = bx * (1 - me_x)
        else:
            src_x = at_x + (bx - HX if ox == 1 else 0)
            dst_x = 0 if ox == 1 else HX + bx
            if arriving:
                dst_x = HX + bx if ox == 1 else 0
            size_x = HX
        src_y, size_y = {0: (8, by), 1: (by, 8), -1: (8, 8)}[oy]
        dst_y = {0: 8, 1: 0, -1: 8 + by}[-oy if arriving else oy]
        if arriving:
            recv = home
        else:
            recv = offsets_x.index(ox if ox in (0, 2) else -ox) * 3 + 1 - oy
        return pltpu.make_async_remote_copy(
            src_ref=window.at[:, pl.ds(src_x, size_x), src_y : src_y + size_y],
            dst_ref=window.at[:, pl.ds(dst_x, size_x), dst_y : dst_y + size_y],
            send_sem=w_send.at[home], recv_sem=w_recv.at[recv],
            device_id=target, device_id_type=MESH), there

    for ox, oy in faces():
        copy, there = face_copy(ox, oy, False)
        guarded(there, copy.start)

    zoff = iota((24, 128), 1)
    zoff = jnp.where(zoff < 96, zoff, zoff - 128)
    row = me_y * half_y - half_y + iota((24, 128), 0)
    z_at = me_z * half_z + zoff
    mask_one = jnp.where(
        (row >= 0) & (row < gy * half_y) & (z_at >= 0) & (z_at < gz * half_z) & (zoff < 64), 1.0, 0.0)
    lane_group = lane >> 5

    def unpack_one(near, own, dst):
        near[(at_one // half_x) * 9 + 4] = own[...]
        for sx in range(min(gx, 3) if not small_x else gx):
            for sy in range(3):
                for q in range(half_x // 4):
                    base = (sx * 3 + sy) * 3
                    low = pltpu.roll(near[base, q], 96, 1)
                    mine = near[base + 1, q]
                    high = pltpu.roll(near[base + 2, q], 32, 1)
                    for j in range(4):
                        piece = jnp.where(
                            lane_group == j, mine,
                            jnp.where(lane_group == (j + 1) % 4, high,
                                      jnp.where(lane_group == (j + 3) % 4, low, 0.0)))
                        if j:
                            piece = pltpu.roll(piece, 128 - 32 * j, 1)
                        dst[sx * half_x + 4 * q + j, 8 * sy : 8 * sy + 8] = piece

    bricks(own_a, near_a, a_send, a_recv, "recv")
    unpack_one(near_a, own_a, mid.diag)

    def plane_ok(start, total):
        if small_x:
            return None
        return lambda x: jnp.where((start + x >= 0) & (start + x < total), 1.0, 0.0)

    mid.scale(lambda x: mid.diag[x], mask_one, plane_ok(me_x * half_x - half_x, gx * half_x))

    lane16 = lane >> 4

    def unpack_two(blocks_in, dst):
        def one(sx, carry):
            for pair in range(gy // 2):
                blocks = []
                for sz in range(gz):
                    first = (sx * gy + 2 * pair) * gz + sz
                    both = jnp.concatenate([blocks_in[first], blocks_in[first + gz]], axis=0)
                    shift = 16 * (sz % 8)
                    blocks.append(pltpu.roll(both, shift, 1) if shift else both)
                for i in range(4):
                    for tile in range((gz + 7) // 8):
                        piece = jnp.zeros((8, 128), F32)
                        for sz in range(8 * tile, min(gz, 8 * tile + 8)):
                            piece = jnp.where(lane16 == (i + sz) % 8, blocks[sz], piece)
                        if i:
                            piece = pltpu.roll(piece, 128 - 16 * i, 1)
                        dst[4 * sx + i, 8 * pair : 8 * pair + 8, 128 * tile : 128 * tile + 128] = piece
            return carry

        lax.fori_loop(0, gx, one, 0)

    def whole_mask(level, rows, lanes):
        shape = (level.rows, level.lanes)
        return jnp.where((iota(shape, 0) < rows) & (iota(shape, 1) < lanes), 1.0, 0.0)

    def restrict(src, dst):
        planes, lanes = dst.shape[0], src.shape[2]
        shape = (lanes, dst.shape[2])
        narrow = ones_where((iota(shape, 0) >> 1) == iota(shape, 1), 0.5)
        sums = [src[2 * i] + src[2 * i + 1] for i in range(planes)]
        out = mm(jnp.concatenate(sums, axis=0), narrow)
        shape = (dst.shape[1], src.shape[1])
        fold = ones_where((iota(shape, 1) >> 1) == iota(shape, 0))
        size = src.shape[1]
        beside_each_other = jnp.concatenate(
            [out[i * size : (i + 1) * size] for i in range(planes)], axis=1)
        out = mm_left(fold, beside_each_other)
        for i in range(planes):
            dst[i] = out[:, i * dst.shape[2] : (i + 1) * dst.shape[2]]

    def prolong(values, rows, wide, dst):
        out = mm(jnp.concatenate(values, axis=0), wide)
        if dst.shape[2] != 128:
            shape = (2 * rows, rows)
            tall = ones_where((iota(shape, 0) >> 1) == iota(shape, 1))
            for i in range(len(values)):
                doubled = mm_left(tall, out[i * rows : (i + 1) * rows])
                for plane in (2 * i + 1, 2 * i + 2):
                    dst[plane, 8 : 8 + 2 * rows] = doubled
            return
        for i in range(len(values)):
            for plane in (2 * i + 1, 2 * i + 2):
                for odd in (0, 1):
                    dst[plane, pl.ds(8 + odd, rows, 2)] = out[i * rows : (i + 1) * rows]

    def widening(above, below):
        shape = (below.lanes, above.lanes)
        return ones_where((iota(shape, 1) >> 1) == iota(shape, 0))

    zoff0 = iota((by + 16, 128), 1)
    zoff0 = jnp.where(zoff0 < 96, zoff0, zoff0 - 128)
    row0 = me_y * by - 8 + iota((by + 16, 128), 0)
    z0 = me_z * bz + zoff0
    mask_zero = jnp.where(
        (row0 >= 0) & (row0 < gy * by) & (z0 >= 0) & (z0 < gz * bz)
        & (zoff0 < bz + 8) & (zoff0 >= -8), 1.0, 0.0)

    for ox, oy in faces():
        copy, there = face_copy(ox, oy, True)
        guarded(there, copy.wait_recv)
    fine.scale(lambda x: window[1, x], mask_zero, plane_ok(me_x * bx - HX, gx * bx))
    fine.init(lambda x: window[0, x])
    fine.down(3)

    pack_one(fine.r, at_x, 8, own_f)
    bricks(own_f, near_f, f_send, f_recv, "start")
    fine.total(0, True)
    everything_a.wait_recv()
    unpack_two(gathered_a, whole_a)
    y2, z2 = gy * half_y // 2, gz * half_z // 2
    restrict(whole_a, a3)
    restrict(a3, a4)
    two.scale(lambda x: whole_a[x], whole_mask(two, y2, z2))
    three.scale(lambda x: a3[x], whole_mask(three, y2 // 2, z2 // 2))
    four.scale(lambda x: a4[x], whole_mask(four, y2 // 4, z2 // 4))
    bricks(own_f, near_f, f_send, f_recv, "recv")
    unpack_one(near_f, own_f, mid.r)
    mid.init(lambda x: mid.r[x])
    mid.down(4)

    sums = jnp.concatenate([halved(mid.r, at_one + 2 * i, 8, half_y // 2) for i in range(4)], axis=1)
    share = mm(sums, to_two)
    pack[...] = share
    gathered[flat_me] = share

    everything = spread(pack, gathered, g_send, g_recv)
    mid.total(2, True)
    everything.wait_recv()
    unpack_two(gathered, whole_f)
    two.init(lambda x: whole_f[x])
    two.down()
    two.total(0, True)
    restrict(two.r, f3)
    three.init(lambda x: f3[x])
    three.down()
    three.total(0, True)
    restrict(three.r, f4)
    four.init(lambda x: f4[x])
    four.down(0, False)
    four.total(0, True)
    prolong([four.v[i, 0 : three.rows // 2] for i in range(four.planes)], three.rows // 2,
            widening(three, four), three.d0)
    three.up()
    three.total_last()
    prolong([three.v[i] for i in range(three.planes)], three.rows, widening(two, three), two.d0)
    two.up()
    two.total_last()

    shape = (two.lanes, 128)
    zoff1 = iota(shape, 1)
    zoff1 = jnp.where(zoff1 < 96, zoff1, zoff1 - 128)
    coarse_z = (me_z * half_z + zoff1) >> 1
    wide = ones_where((iota(shape, 0) == coarse_z) & (iota(shape, 0) < z2))
    shape = (mid.rows, two.rows)
    coarse_y = (me_y * half_y - half_y + iota(shape, 0)) >> 1
    tall = ones_where(iota(shape, 1) == coarse_y)
    values = []
    for i in range(mid.planes // 2):
        if small_x:
            values.append(two.v[i])
        else:
            at = me_x * (half_x // 2) - half_x // 2 + i
            inside = (at >= 0) & (at < two.planes)
            values.append(two.v[jnp.clip(at, 0, two.planes - 1)] * jnp.where(inside, 1.0, 0.0))
    out = mm(jnp.concatenate(values, axis=0), wide)
    size = two.rows
    out = mm_left(tall, jnp.concatenate(
        [out[i * size : (i + 1) * size] for i in range(len(values))], axis=1))
    for i in range(len(values)):
        spread_out = out[:, 128 * i : 128 * i + 128]
        mid.d0[2 * i + 1, 8 : 8 + mid.rows] = spread_out
        mid.d0[2 * i + 2, 8 : 8 + mid.rows] = spread_out
    mid.up(2)
    mid.total_last(2)

    shape = (128, 128)
    lane0 = iota(shape, 1)
    from_lane = jnp.where(lane0 < 96, lane0 >> 1, 64 + (lane0 >> 1))
    wide = ones_where((iota(shape, 0) == from_lane) & ((lane0 < bz + 8) | (lane0 >= 120)))
    at = (bx // 2 - HX // 2) * me_x if small_x else bx // 2 - HX // 2
    rows = fine.rows // 2
    prolong([mid.v[at + i, 4 : 4 + rows] for i in range(fine.planes // 2)], rows, wide, fine.d0)
    fine.up(1, True)
    p_ref[...] = (fine.v[pl.ds(at_x, bx), 8 : 8 + by]
                  + fine.d0[pl.ds(at_x + 1, bx), 16 : 16 + by])[:, :, 0:bz]
    e_ref[...] = fine.r[pl.ds(at_x, bx), 8 : 8 + by, 0:bz]

    pl.when(has_high)(lambda: z_copy(1).wait_send())
    pl.when(has_low)(lambda: z_copy(0).wait_send())
    bricks(own_a, near_a, a_send, a_recv, "send")
    bricks(own_f, near_f, f_send, f_recv, "send")
    for ox, oy in faces():
        copy, there = face_copy(ox, oy, False)
        guarded(there, copy.wait_send)
    everything.wait_send()
    everything_a.wait_send()


def hand_on(p_ref, e_ref, pressure_ref, residual_ref):
    pressure_ref[...] = p_ref[...]
    residual_ref[...] = e_ref[...]


def shards(counts, right_side, diagonal):
    gx, gy, gz = counts
    bx, by, bz = right_side.shape
    slots_x = min(gx, 2) if gx <= 2 else 3
    x0 = bx + (HX * (gx - 1) if gx <= 2 else 2 * HX)

    def lanes_for(size):
        return 128 * ((size + 128) // 128)

    def level(planes, rows, lanes):
        plain = pltpu.VMEM((planes, rows, lanes), F32)
        padded = pltpu.VMEM((planes + 2, rows + 16, lanes), F32)
        return [plain] * 4 + [padded] * 3

    two = (gx * bx // 4, gy * by // 4, lanes_for(gz * bz // 4))
    three = (gx * bx // 8, gy * by // 8, lanes_for(gz * bz // 8))
    four = (gx * bx // 16, max(8, gy * by // 16), lanes_for(gz * bz // 16))
    brick = (bx // 8, by // 2, 128)
    near = (slots_x * 9,) + brick
    scratch = [
        pltpu.VMEM((128, 2 * bx * by), F32),
        pltpu.VMEM((2, x0, by + 16, 128), F32),
        pltpu.VMEM(near, F32),
        pltpu.VMEM(near, F32),
        pltpu.VMEM(brick, F32),
        pltpu.VMEM(brick, F32),
        pltpu.VMEM((by // 4, 128), F32),
        pltpu.VMEM((gx * gy * gz, by // 4, 128), F32),
        pltpu.VMEM((by // 4, 128), F32),
        pltpu.VMEM((gx * gy * gz, by // 4, 128), F32),
        pltpu.VMEM(two, F32),
        pltpu.VMEM(two, F32),
        pltpu.VMEM(three, F32),
        pltpu.VMEM(three, F32),
        pltpu.VMEM(four, F32),
        pltpu.VMEM(four, F32),
    ]
    scratch += level(x0, by + 16, 128)
    scratch += level(slots_x * bx // 2, 24, 128)
    scratch += level(*two) + level(*three) + level(*four)
    dma = pltpu.SemaphoreType.DMA
    scratch += [dma((2,)), dma((2,))]
    scratch += [dma((slots_x * 3,))] * 2
    scratch += [dma((slots_x * 9,))] * 4
    scratch += [dma] * 4
    out = jax.ShapeDtypeStruct(right_side.shape, F32)
    vmem = pl.BlockSpec(memory_space=pltpu.VMEM)
    results = pl.pallas_call(
        functools.partial(kernel, counts),
        out_shape=(out, out),
        in_specs=[vmem, vmem],
        out_specs=(vmem, vmem),
        scratch_shapes=scratch,
        compiler_params=pltpu.CompilerParams(
            collective_id=0, has_side_effects=True, vmem_limit_bytes=56 * 1024 * 1024
        ),
    )(right_side, diagonal)
    return pl.pallas_call(
        hand_on, out_shape=(out, out), in_specs=[vmem, vmem], out_specs=(vmem, vmem)
    )(*results)


def solution(mesh):
    spec = P("gx", "gy", "gz")
    counts = tuple(mesh.shape[name] for name in ("gx", "gy", "gz"))
    return jax.shard_map(
        functools.partial(shards, counts), mesh=mesh, in_specs=(spec, spec),
        out_specs=(spec, spec), check_vma=False)
```
